32 devices in a mesh: pos: 16 (over z, y, x), head: 2 (over core).
Axes of the slice: x: 2, y: 2, z: 4, core: 2. Of those that a mesh axis runs over, the one named last changes fastest.
Arguments:
- inputs: bfloat16 [16384, 1024], P('pos'), may hold values from -400 to 400
- valid_blocks: int32 [128], P('pos'), may hold values from 0 to 1, as said below
- latents: bfloat16 [2048, 1024], P('pos'), may hold values from -6 to 6
- w_query: bfloat16 [1024, 1024], P(None, 'head'), may hold values from -0.1875 to 0.1875
- w_key: bfloat16 [1024, 1024], P(None, 'head'), may hold values from -0.1875 to 0.1875
- w_value: bfloat16 [1024, 1024], P(None, 'head'), may hold values from -0.1875 to 0.1875
- w_out: bfloat16 [1024, 1024], P('head'), may hold values from -0.1875 to 0.1875
- w_mlp: bfloat16 [1024, 1024], replicated, may hold values from -0.1875 to 0.1875
- w_lkey: bfloat16 [1024, 1024], P(None, 'head'), may hold values from -0.1875 to 0.1875
- w_lvalue: bfloat16 [1024, 1024], P(None, 'head'), may hold values from -0.1875 to 0.1875
- w_pquery: bfloat16 [1024, 1024], P(None, 'head'), may hold values from -0.1875 to 0.1875
- w_pout: bfloat16 [1024, 1024], P('head'), may hold values from -0.1875 to 0.1875
Outputs:
- decoded: bfloat16 [16384, 1024], P(('pos', 'head'))
The draws below stay inside these ranges and needn't reach their ends.
Inputs may be any that keep to these rules, and one draw needn't show every extreme that they name: `valid_blocks`: within the 1024 positions of each device the blocks marked 1 come first; every device has at least one block marked 1, and some device has all its blocks marked 1.
All inputs are finite; a program needn't handle non-finite values.
Results may differ from the reference program's by a relative error of at most 0.017.
The reference program's roundings to bfloat16 on the way count: a program that leaves them out, or rounds other values in their place, can miss the bound.
Values may be sent and summed in bfloat16 or wider, within the bound.
A program may use at most 128 MiB of HBM per device.

```python
import jax
import jax.numpy as jnp
from jax import lax

D = 1024
HEADS = 8
HEAD_DIM = 128
LAT = 2048
POS_DEV = 1024
BLK = 128
INNER = 1024
N_POS = 16


def draw_inputs(key, part):
    key_base = jax.random.fold_in(key, 11)
    normal_part = jax.random.truncated_normal(key_base, -6.0, 6.0, (POS_DEV * N_POS, D), jnp.float32)
    return normal_part.astype(jnp.bfloat16)


def draw_valid_blocks(key, part):
    blocks_each = POS_DEV // BLK
    key_counts = jax.random.fold_in(key, 21)
    key_full = jax.random.fold_in(key, 22)
    counts = jax.random.randint(key_counts, (N_POS,), 1, blocks_each + 1)
    fullest = jax.random.randint(key_full, (), 0, N_POS)
    counts = jnp.where(jnp.arange(N_POS) == fullest, blocks_each, counts)
    marks = jnp.arange(blocks_each)[None, :] < counts[:, None]
    return marks.astype(jnp.int32).reshape(N_POS * blocks_each)


def shard_levels(key, shape, split, least, high):
    def one(dim, shards_of):
        heights = jax.random.uniform(jax.random.fold_in(jax.random.fold_in(key, 6), dim), (shards_of,), jnp.float32, least / len(split), high / len(split))
        return jnp.repeat(jnp.exp(heights), shape[dim] // shards_of).reshape((-1,) + (1,) * (len(shape) - dim - 1))

    loudness = one(*split[0])
    for cut in split[1:]:
        loudness = loudness * one(*cut)
    return loudness


def scatter_about(key, extent, spread, most, pieces=(), held_as=jnp.bfloat16):
    loudness = shard_levels(key, extent, pieces, -0.22, 0.18) if pieces else 1.0
    result = jax.random.normal(key, extent, jnp.float32) * spread * loudness
    return jnp.minimum(jnp.maximum(result, -most), most).astype(held_as)


def setup_inputs(seed: int = 0) -> dict:
    key_of = jax.random.split(jax.random.key(seed), 13)
    inputs = draw_inputs(jax.random.fold_in(key_of[12], 71), 0)
    valid_blocks = draw_valid_blocks(jax.random.fold_in(key_of[12], 71), 0)
    latents = scatter_about(key_of[2], (LAT, D), 1.0, 6.0, ((0, 16),))
    w_query = scatter_about(key_of[3], (D, INNER), D ** -0.5, 0.1875, ((1, 2),))
    w_key = scatter_about(key_of[4], (D, INNER), D ** -0.5, 0.1875, ((1, 2),))
    w_value = scatter_about(key_of[5], (D, INNER), D ** -0.5, 0.1875, ((1, 2),))
    w_out = scatter_about(key_of[6], (INNER, D), INNER ** -0.5, 0.1875, ((0, 2),))
    w_mlp = scatter_about(key_of[7], (D, D), D ** -0.5, 0.1875)
    w_lkey = scatter_about(key_of[8], (D, INNER), D ** -0.5, 0.1875, ((1, 2),))
    w_lvalue = scatter_about(key_of[9], (D, INNER), D ** -0.5, 0.1875, ((1, 2),))
    w_pquery = scatter_about(key_of[10], (D, INNER), D ** -0.5, 0.1875, ((1, 2),))
    w_pout = scatter_about(key_of[11], (INNER, D), INNER ** -0.5, 0.1875, ((0, 2),))
    return {"inputs": inputs, "valid_blocks": valid_blocks, "latents": latents, "w_query": w_query, "w_key": w_key, "w_value": w_value, "w_out": w_out, "w_mlp": w_mlp, "w_lkey": w_lkey, "w_lvalue": w_lvalue, "w_pquery": w_pquery, "w_pout": w_pout}


masked_score = -1e+30
epsilon = 1e-05

def rms_norm(values):
    return values * lax.rsqrt(lax.optimization_barrier(jnp.mean(values * values, axis=-1, keepdims=True)) + epsilon)

def widen(values):
    return lax.optimization_barrier(values).astype(jnp.float32)

def reference(inputs, valid_blocks, latents, w_query, w_key, w_value, w_out, w_mlp, w_lkey, w_lvalue, w_pquery, w_pout):
    scaling = HEAD_DIM ** (-0.5)
    positions = inputs.shape[0]
    inner = HEADS * HEAD_DIM
    pos_keys = widen(jnp.dot(inputs, w_key, preferred_element_type=jnp.float32).astype(jnp.bfloat16)).reshape(positions, HEADS, HEAD_DIM)
    pos_values = widen(jnp.dot(inputs, w_value, preferred_element_type=jnp.float32).astype(jnp.bfloat16)).reshape(positions, HEADS, HEAD_DIM)
    alive_mask = jnp.repeat(valid_blocks, BLK) > 0
    lat_block = min(LAT, 128)
    lat_queries = widen(jnp.dot(latents, w_query, preferred_element_type=jnp.float32).astype(jnp.bfloat16))
    lat_queries = lat_queries.reshape(LAT // lat_block, lat_block, HEADS, HEAD_DIM)

    def cross_block(query_rows):
        scores = jnp.einsum('lhe,phe->lhp', query_rows, pos_keys) * scaling
        scores = jnp.where(alive_mask[None, None, :], scores, masked_score)
        row_max = lax.optimization_barrier(jnp.max(scores, axis=-1, keepdims=True))
        exponent = jnp.exp(scores - row_max)
        totals = lax.optimization_barrier(jnp.sum(exponent, axis=-1))
        weights = widen(exponent.astype(jnp.bfloat16))
        numerators = jnp.einsum('lhp,phe->lhe', weights, pos_values)
        return (numerators / totals[..., None]).astype(jnp.bfloat16).reshape(lat_block, inner)
    attended = lax.map(cross_block, lat_queries).reshape(LAT, inner)
    merged = jnp.dot(attended, w_out, preferred_element_type=jnp.float32)
    normed = rms_norm(merged)
    hidden = jax.nn.gelu(jnp.dot(normed.astype(jnp.bfloat16), w_mlp, preferred_element_type=jnp.float32))
    lat_rows = (normed + hidden).astype(jnp.bfloat16)
    lat_keys = widen(jnp.dot(lat_rows, w_lkey, preferred_element_type=jnp.float32).astype(jnp.bfloat16)).reshape(LAT, HEADS, HEAD_DIM)
    lat_values = widen(jnp.dot(lat_rows, w_lvalue, preferred_element_type=jnp.float32).astype(jnp.bfloat16)).reshape(LAT, HEADS, HEAD_DIM)
    pos_block = min(positions, 512)
    pos_queries = widen(jnp.dot(inputs, w_pquery, preferred_element_type=jnp.float32).astype(jnp.bfloat16))
    pos_queries = pos_queries.reshape(positions // pos_block, pos_block, HEADS, HEAD_DIM)

    def decode_block(query_rows):
        scores = jnp.einsum('phe,lhe->phl', query_rows, lat_keys) * scaling
        row_max = lax.optimization_barrier(jnp.max(scores, axis=-1, keepdims=True))
        exponent = jnp.exp(scores - row_max)
        totals = lax.optimization_barrier(jnp.sum(exponent, axis=-1))
        weights = widen(exponent.astype(jnp.bfloat16))
        numerators = jnp.einsum('phl,lhe->phe', weights, lat_values)
        return (numerators / totals[..., None]).astype(jnp.bfloat16).reshape(pos_block, inner)
    pos_attended = lax.map(decode_block, pos_queries).reshape(positions, inner)
    final = jnp.dot(pos_attended, w_pout, preferred_element_type=jnp.float32)
    return rms_norm(final).astype(jnp.bfloat16)
```

```python
import functools
import math

import jax
import jax.numpy as jnp
from jax import lax
from jax.experimental import pallas as pl
from jax.experimental.pallas import tpu as pltpu
from jax.sharding import PartitionSpec as P

HEAD_DIM = 128
masked_score = -1e30
epsilon = 1e-05
F32 = jnp.float32
BF16 = jnp.bfloat16
MESH = pl.DeviceIdType.MESH
N_STREAMS = 2


def rms_norm(values):
    return values * lax.rsqrt(jnp.mean(values * values, axis=-1, keepdims=True) + epsilon)


def mm(a, b):
    return jnp.dot(a, b, preferred_element_type=F32)


def group(g):
    return (0, 1) if g == 0 else (2 ** (g - 1), 2**g)


def kernel(n, inputs, bias, latents, w_query, w_key, w_value, w_out, w_mlp, w_lkey, w_lvalue,
           w_pquery, w_pout, out,
           v_in, v_bias, v_lat, v_wq, v_wk, v_wv, v_wo, v_wm, v_wlk, v_wlv, v_wpq, v_wpo,
           qt, keys, valt, pqt, osum, stats, orecv, srecv, lr, lkeys, lvalt, pa,
           tsend, trecv, msend, mrecv,
           load_sem, gs_sem, gr_sem, hs_sem, hr_sem, ds_sem, dr_sem,
           os_sem, or_sem, ss_sem, sr_sem, x_sem):
    bits = n.bit_length() - 1
    heads, pos, _ = keys.shape
    hs = heads // N_STREAMS
    lat_local = v_lat.shape[0]
    lat = n * lat_local
    width = v_lat.shape[1]
    scale = HEAD_DIM ** (-0.5) * math.log2(math.e)
    me = lax.axis_index("pos")
    core = lax.axis_index("head")
    high = list(range(bits - 1, 1, -1))
    gather_order = [high + [0, 1], high + [1, 0]]
    reduce_order = [high + [1, 0], high + [0, 1]]

    def partner(bit):
        step = 2**bit
        flipped = me + step - 2 * step * ((me // step) % 2)
        return {"pos": flipped, "head": core}

    other = {"pos": me, "head": 1 - core}

    loads = []
    for i, (src, dst) in enumerate([
        (latents, v_lat), (w_query, v_wq), (inputs, v_in), (w_key, v_wk), (w_value, v_wv),
        (bias, v_bias), (w_pquery, v_wpq), (w_out, v_wo), (w_mlp, v_wm), (w_lkey, v_wlk),
        (w_lvalue, v_wlv), (w_pout, v_wpo),
    ]):
        copy = pltpu.make_async_copy(src, dst, load_sem.at[i])
        copy.start()
        loads.append(copy)

    barrier = pltpu.get_barrier_semaphore()
    for bit in range(bits):
        pl.semaphore_signal(barrier, inc=1, device_id=partner(bit), device_id_type=MESH)
    pl.semaphore_signal(barrier, inc=1, device_id=other, device_id_type=MESH)
    pl.semaphore_wait(barrier, bits + 1)

    def remote(src, dst, send, recv, device):
        return pltpu.make_async_remote_copy(
            src_ref=src, dst_ref=dst, send_sem=send, recv_sem=recv, device_id=device,
            device_id_type=MESH)

    class Gather:
        def __init__(self, view, send, recv):
            self.copies = {}
            for s in range(N_STREAMS):
                for t in range(bits):
                    for g in range(t + 1):
                        a, b = group(g)
                        self.copies[s, t, g] = remote(
                            view(s, a, b), view(s, 2**t + a, 2**t + b),
                            send.at[s, t, g], recv.at[s, t, g], partner(gather_order[s][t]))

        def ready(self, g):
            for s in range(N_STREAMS):
                if g > 0:
                    for i in range(g):
                        self.copies[s, g - 1, i].wait_recv()
                for t in range(g, bits):
                    self.copies[s, t, g].start()

        def finish(self):
            for copy in self.copies.values():
                copy.wait_send()

    loads[0].wait()
    loads[1].wait()
    own = mm(v_lat[...], v_wq[...]).T.astype(BF16)
    for h in range(heads):
        qt[h // hs, 0, h % hs] = own[h * HEAD_DIM:(h + 1) * HEAD_DIM]
    gather_q = Gather(lambda s, a, b: qt.at[s, a:b], gs_sem, gr_sem)
    gather_q.ready(0)

    rows = min(pos, 256)

    def project(weight, store):
        def body(i, _):
            start = pl.multiple_of(i * rows, rows)
            store(start, mm(v_in[pl.ds(start, rows)], weight[...]))
            return 0
        lax.fori_loop(0, pos // rows, body, 0)

    def store_keys(start, value):
        for h in range(heads):
            keys[h, pl.ds(start, rows)] = value[:, h * HEAD_DIM:(h + 1) * HEAD_DIM].astype(BF16)

    def store_transposed(dst):
        def store(start, value):
            flipped = value.T.astype(BF16)
            for h in range(heads):
                dst[h, :, pl.ds(start, rows)] = flipped[h * HEAD_DIM:(h + 1) * HEAD_DIM]
        return store

    loads[2].wait()
    loads[3].wait()
    project(v_wk, store_keys)
    gather_q.ready(1)
    loads[4].wait()
    project(v_wv, store_transposed(valt))
    gather_q.ready(2)

    def attend(key, query, value, extra):
        scores = mm(key, query) * scale
        if extra is not None:
            scores = scores + extra
        top = jnp.max(scores, axis=0, keepdims=True)
        exponent = jnp.exp2(scores - top)
        total = jnp.sum(exponent, axis=0, keepdims=True)
        return top, total, mm(value, exponent.astype(BF16))

    pair = 2 if lat_local % 128 == 0 else 1
    quarter = n // 4

    def encode(q):
        target = {0: 0, 1: 2, 2: 1, 3: 3}[q]

        def body(i, _):
            h = i % heads
            r = (i // heads) * pair
            s, hh = h // hs, h % hs
            src, dst = q * quarter + r, target * quarter + r
            query = [qt[s, src + j, hh] for j in range(pair)]
            extra = [v_bias[...]] * pair
            top, total, summed = attend(
                keys[h], jnp.concatenate(query, axis=1) if pair > 1 else query[0],
                valt[h], jnp.concatenate(extra, axis=1) if pair > 1 else extra[0])
            summed = summed.astype(BF16)
            for j in range(pair):
                cut = slice(j * lat_local, (j + 1) * lat_local)
                osum[s, dst + j, hh] = summed[:, cut]
                stats[s, dst + j, hh, 0:1] = top[:, cut]
                stats[s, dst + j, hh, 1:2] = total[:, cut]
            return 0

        lax.fori_loop(0, heads * quarter // pair, body, 0)

    sent = []

    def reduce_copies(t, part, a, b, base):
        copies = []
        for s in range(N_STREAMS):
            device = partner(reduce_order[s][t])
            copies.append((
                remote(osum.at[s, a:b], orecv.at[s, base:base + b - a],
                       os_sem.at[s, t, part], or_sem.at[s, t, part], device),
                remote(stats.at[s, a:b], srecv.at[s, base:base + b - a],
                       ss_sem.at[s, t, part], sr_sem.at[s, t, part], device)))
        for o, st in copies:
            o.start()
            st.start()
        sent.extend(copies)
        return copies

    def merge(copies, a, b, base):
        for o, st in copies:
            o.wait_recv()
            st.wait_recv()

        def body(i, _):
            h = i % heads
            r = i // heads
            s, hh = h // hs, h % hs
            mine, theirs = stats[s, a + r, hh], srecv[s, base + r, hh]
            top = jnp.maximum(mine[0:1], theirs[0:1])
            f, g = jnp.exp2(mine[0:1] - top), jnp.exp2(theirs[0:1] - top)
            stats[s, a + r, hh, 0:1] = top
            stats[s, a + r, hh, 1:2] = mine[1:2] * f + theirs[1:2] * g
            osum[s, a + r, hh] = (
                osum[s, a + r, hh].astype(F32) * f + orecv[s, base + r, hh].astype(F32) * g
            ).astype(BF16)
            return 0

        lax.fori_loop(0, heads * (b - a), body, 0)

    loads[5].wait()
    encode(0)
    gather_q.ready(3)
    for g in range(4, bits):
        gather_q.ready(g)
    if bits == 4:
        encode(1)
        early = reduce_copies(3, 0, 2 * quarter, 3 * quarter, quarter)
        gather_q.ready(bits)
    else:
        gather_q.ready(bits)
        encode(1)
        early = reduce_copies(bits - 1, 0, 2 * quarter, 3 * quarter, quarter)
    encode(3)
    late = reduce_copies(bits - 1, 1, 3 * quarter, n, 0)
    encode(2)
    merge(late, quarter, 2 * quarter, 0)
    base = 2 * quarter
    step = reduce_copies(bits - 2, 0, quarter, 2 * quarter, base)
    loads[6].wait()
    project(v_wpq, store_transposed(pqt))
    merge(early, 0, quarter, quarter)
    merge(step, 0, quarter, base)
    base += quarter
    for t in range(bits - 3, -1, -1):
        step = reduce_copies(t, 0, 2**t, 2 ** (t + 1), base)
        merge(step, 0, 2**t, base)
        base += 2**t
    gather_q.finish()

    attended = []
    for h in range(heads):
        s, hh = h // hs, h % hs
        attended.append((osum[s, 0, hh].astype(F32) / stats[s, 0, hh][1:2]).T.astype(BF16))
    loads[7].wait()
    partial = mm(jnp.concatenate(attended, axis=1), v_wo[...]).astype(BF16)
    msend[...] = partial
    swap = remote(msend, mrecv, x_sem.at[0], x_sem.at[1], other)
    swap.start()
    loads[8].wait()
    swap.wait()
    normed = rms_norm(msend[...].astype(F32) + mrecv[...].astype(F32))
    hidden = jax.nn.gelu(mm(normed.astype(BF16), v_wm[...]))
    lat_rows = (normed + hidden).astype(BF16)
    parts = lr.shape[0]
    span = width // parts
    for q in range(parts):
        lr[q, 0] = lat_rows[:, q * span:(q + 1) * span]

    gather_l = Gather(lambda s, a, b: lr.at[core * N_STREAMS + s, a:b], hs_sem, hr_sem)
    gather_l.ready(0)
    shares = {}
    for g in range(1, bits + 1):
        gather_l.ready(g)
        a, b = group(g)
        for s in range(N_STREAMS):
            view = lr.at[core * N_STREAMS + s, a:b]
            shares[s, g] = remote(view, view, ds_sem.at[s, g], dr_sem.at[s, g], other)
            shares[s, g].start()
        if g == 1:
            loads[9].wait()
            loads[10].wait()
    for copy in shares.values():
        copy.wait_recv()

    block = lat // 4

    def latent_kv(q):
        acc_k = acc_v = None
        for part in range(parts):
            held = q if part % N_STREAMS == 0 else {0: 0, 1: 2, 2: 1, 3: 3}[q]
            x = lr[part, held * quarter:(held + 1) * quarter].reshape(block, span)
            k = mm(x, v_wlk[part * span:(part + 1) * span])
            v = mm(x, v_wlv[part * span:(part + 1) * span])
            acc_k = k if acc_k is None else acc_k + k
            acc_v = v if acc_v is None else acc_v + v
        flipped = acc_v.T.astype(BF16)
        for h in range(heads):
            cut = slice(h * HEAD_DIM, (h + 1) * HEAD_DIM)
            lkeys[h, q * block:(q + 1) * block] = acc_k[:, cut].astype(BF16)
            lvalt[h, :, q * block:(q + 1) * block] = flipped[cut]

    for q in range(4):
        latent_kv(q)

    def decode(i, _):
        h = i % heads
        start = pl.multiple_of((i // heads) * rows, rows)
        _, total, summed = attend(lkeys[h], pqt[h, :, pl.ds(start, rows)], lvalt[h], None)
        pa[h, pl.ds(start, rows)] = (summed / total).T.astype(BF16)
        return 0

    half = pos // 2
    loads[11].wait()

    def terms(start, size):
        joined = jnp.concatenate([pa[h, pl.ds(start, size)] for h in range(heads)], axis=1)
        return mm(joined, v_wpo[...])

    per_half = half // rows
    theirs = (1 - core) * per_half
    mine = core * per_half
    swaps = []
    for i in range(per_half):
        lax.fori_loop((theirs + i) * heads, (theirs + i + 1) * heads, decode, 0)
        start = pl.multiple_of((theirs + i) * rows, rows)
        tsend[i] = terms(start, rows).astype(BF16)
        copy = remote(tsend.at[i], trecv.at[i], x_sem.at[2 + 2 * i], x_sem.at[3 + 2 * i], other)
        copy.start()
        swaps.append(copy)
    for i in range(per_half):
        lax.fori_loop((mine + i) * heads, (mine + i + 1) * heads, decode, 0)
        start = pl.multiple_of((mine + i) * rows, rows)
        own_terms = terms(start, rows).astype(BF16).astype(F32)
        swaps[i].wait_recv()
        out[i * rows:(i + 1) * rows] = rms_norm(own_terms + trecv[i].astype(F32)).astype(BF16)
    for copy in swaps:
        copy.wait_send()
    for o, st in sent:
        o.wait_send()
        st.wait_send()
    gather_l.finish()
    for copy in shares.values():
        copy.wait_send()


def per_device(n, inputs, valid_blocks, latents, *weights):
    pos, width = inputs.shape
    lat_local = latents.shape[0]
    columns = weights[0].shape[1]
    heads = columns // HEAD_DIM
    hs = heads // N_STREAMS
    lat = n * lat_local
    bits = n.bit_length() - 1
    rows = min(pos, 256)
    per_half = pos // 2 // rows
    block = pos // valid_blocks.shape[0]
    bias = jnp.where(jnp.repeat(valid_blocks, block) > 0, 0.0, masked_score).astype(F32)
    bias = jnp.broadcast_to(bias[:, None], (pos, lat_local))
    operands = (inputs, bias, latents) + weights
    landed = [pltpu.VMEM(a.shape, a.dtype) for a in operands]
    dma = pltpu.SemaphoreType.DMA
    n_recv = n
    scratch = landed + [
        pltpu.VMEM((N_STREAMS, n, hs, HEAD_DIM, lat_local), BF16),
        pltpu.VMEM((heads, pos, HEAD_DIM), BF16),
        pltpu.VMEM((heads, HEAD_DIM, pos), BF16),
        pltpu.VMEM((heads, HEAD_DIM, pos), BF16),
        pltpu.VMEM((N_STREAMS, n, hs, HEAD_DIM, lat_local), BF16),
        pltpu.VMEM((N_STREAMS, n, hs, 2, lat_local), F32),
        pltpu.VMEM((N_STREAMS, n_recv, hs, HEAD_DIM, lat_local), BF16),
        pltpu.VMEM((N_STREAMS, n_recv, hs, 2, lat_local), F32),
        pltpu.VMEM((2 * N_STREAMS, n, lat_local, width // (2 * N_STREAMS)), BF16),
        pltpu.VMEM((heads, lat, HEAD_DIM), BF16),
        pltpu.VMEM((heads, HEAD_DIM, lat), BF16),
        pltpu.VMEM((heads, pos, HEAD_DIM), BF16),
        pltpu.VMEM((per_half, rows, width), BF16),
        pltpu.VMEM((per_half, rows, width), BF16),
        pltpu.VMEM((lat_local, width), BF16),
        pltpu.VMEM((lat_local, width), BF16),
        dma((len(operands),)),
        dma((N_STREAMS, bits, bits)),
        dma((N_STREAMS, bits, bits)),
        dma((N_STREAMS, bits, bits)),
        dma((N_STREAMS, bits, bits)),
        dma((N_STREAMS, bits + 1)),
        dma((N_STREAMS, bits + 1)),
        dma((N_STREAMS, bits, 2)),
        dma((N_STREAMS, bits, 2)),
        dma((N_STREAMS, bits, 2)),
        dma((N_STREAMS, bits, 2)),
        dma((2 + 2 * per_half,)),
    ]
    return pl.pallas_call(
        functools.partial(kernel, n),
        out_shape=jax.ShapeDtypeStruct((pos // 2, width), BF16),
        in_specs=[pl.BlockSpec(memory_space=pl.ANY)] * len(operands),
        out_specs=pl.BlockSpec(memory_space=pltpu.VMEM),
        scratch_shapes=scratch,
        compiler_params=pltpu.CompilerParams(
            collective_id=0, has_side_effects=True, vmem_limit_bytes=60 * 1024 * 1024),
        name="perceiver",
    )(*operands)


def solution(mesh):
    placed = (
        P("pos", None),
        P("pos"),
        P("pos", None),
        P(None, "head"),
        P(None, "head"),
        P(None, "head"),
        P("head", None),
        P(),
        P(None, "head"),
        P(None, "head"),
        P(None, "head"),
        P("head", None),
    )
    return jax.shard_map(
        functools.partial(per_device, mesh.shape["pos"]), mesh=mesh, in_specs=placed,
        out_specs=P(("pos", "head"), None), check_vma=False
    )
```

```python
import functools
import math

import jax
import jax.numpy as jnp
from jax import lax
from jax.experimental import pallas as pl
from jax.experimental.pallas import tpu as pltpu
from jax.sharding import PartitionSpec as P

HEAD_DIM = 128
masked_score = -1e30
epsilon = 1e-05
F32 = jnp.float32
BF16 = jnp.bfloat16
MESH = pl.DeviceIdType.MESH
N_STREAMS = 2


def rms_norm(values):
    return values * lax.rsqrt(jnp.mean(values * values, axis=-1, keepdims=True) + epsilon)


def mm(a, b):
    return jnp.dot(a, b, preferred_element_type=F32)


def group(g):
    return (0, 1) if g == 0 else (2 ** (g - 1), 2**g)


def kernel(n, inputs, bias, latents, w_query, w_key, w_value, w_out, w_mlp, w_lkey, w_lvalue,
           w_pquery, w_pout, out,
           v_in, v_bias, v_lat, v_wq, v_wk, v_wv, v_wo, v_wm, v_wlk, v_wlv, v_wpq, v_wpo,
           qt, keys, valt, pqt, osum, stats, orecv, srecv, lr, lkeys, lvalt, pa, dstat, dsum,
           tsend, trecv, msend, mrecv,
           load_sem, gs_sem, gr_sem, hs_sem, hr_sem, ds_sem, dr_sem,
           os_sem, or_sem, ss_sem, sr_sem, x_sem):
    bits = n.bit_length() - 1
    heads, pos, _ = keys.shape
    hs = heads // N_STREAMS
    lat_local = v_lat.shape[0]
    lat = n * lat_local
    width = v_lat.shape[1]
    scale = HEAD_DIM ** (-0.5) * math.log2(math.e)
    me = lax.axis_index("pos")
    core = lax.axis_index("head")
    high = list(range(bits - 1, 1, -1))
    gather_order = [high + [0, 1], high + [1, 0]]
    reduce_order = [high + [1, 0], high + [0, 1]]

    def partner(bit):
        step = 2**bit
        flipped = me + step - 2 * step * ((me // step) % 2)
        return {"pos": flipped, "head": core}

    other = {"pos": me, "head": 1 - core}

    loads = []
    for i, (src, dst) in enumerate([
        (latents, v_lat), (w_query, v_wq), (inputs, v_in), (w_key, v_wk), (w_value, v_wv),
        (bias, v_bias), (w_pquery, v_wpq), (w_out, v_wo), (w_mlp, v_wm), (w_lkey, v_wlk),
        (w_lvalue, v_wlv), (w_pout, v_wpo),
    ]):
        copy = pltpu.make_async_copy(src, dst, load_sem.at[i])
        copy.start()
        loads.append(copy)

    barrier = pltpu.get_barrier_semaphore()
    for bit in range(bits):
        pl.semaphore_signal(barrier, inc=1, device_id=partner(bit), device_id_type=MESH)
    pl.semaphore_signal(barrier, inc=1, device_id=other, device_id_type=MESH)
    pl.semaphore_wait(barrier, bits + 1)

    def remote(src, dst, send, recv, device):
        return pltpu.make_async_remote_copy(
            src_ref=src, dst_ref=dst, send_sem=send, recv_sem=recv, device_id=device,
            device_id_type=MESH)

    class Gather:
        def __init__(self, view, send, recv):
            self.copies = {}
            for s in range(N_STREAMS):
                for t in range(bits):
                    for g in range(t + 1):
                        a, b = group(g)
                        self.copies[s, t, g] = remote(
                            view(s, a, b), view(s, 2**t + a, 2**t + b),
                            send.at[s, t, g], recv.at[s, t, g], partner(gather_order[s][t]))

        def ready(self, g):
            for s in range(N_STREAMS):
                if g > 0:
                    for i in range(g):
                        self.copies[s, g - 1, i].wait_recv()
                for t in range(g, bits):
                    self.copies[s, t, g].start()

        def finish(self):
            for copy in self.copies.values():
                copy.wait_send()

    loads[0].wait()
    loads[1].wait()
    own = mm(v_lat[...], v_wq[...]).T.astype(BF16)
    for h in range(heads):
        qt[h // hs, 0, h % hs] = own[h * HEAD_DIM:(h + 1) * HEAD_DIM]
    gather_q = Gather(lambda s, a, b: qt.at[s, a:b], gs_sem, gr_sem)
    gather_q.ready(0)

    rows = min(pos, 256)

    def project(weight, store):
        def body(i, _):
            start = pl.multiple_of(i * rows, rows)
            store(start, mm(v_in[pl.ds(start, rows)], weight[...]))
            return 0
        lax.fori_loop(0, pos // rows, body, 0)

    def store_keys(start, value):
        for h in range(heads):
            keys[h, pl.ds(start, rows)] = value[:, h * HEAD_DIM:(h + 1) * HEAD_DIM].astype(BF16)

    def store_transposed(dst):
        def store(start, value):
            flipped = value.T.astype(BF16)
            for h in range(heads):
                dst[h, :, pl.ds(start, rows)] = flipped[h * HEAD_DIM:(h + 1) * HEAD_DIM]
        return store

    loads[2].wait()
    loads[3].wait()
    project(v_wk, store_keys)
    gather_q.ready(1)
    loads[4].wait()
    project(v_wv, store_transposed(valt))
    gather_q.ready(2)

    def attend(key, query, value, extra):
        scores = mm(key, query) * scale
        if extra is not None:
            scores = scores + extra
        top = jnp.max(scores, axis=0, keepdims=True)
        exponent = jnp.exp2(scores - top)
        total = jnp.sum(exponent, axis=0, keepdims=True)
        return top, total, mm(value, exponent.astype(BF16))

    pair = 2 if lat_local % 128 == 0 else 1
    quarter = n // 4

    def encode(q):
        target = {0: 0, 1: 2, 2: 1, 3: 3}[q]

        def body(i, _):
            h = i % heads
            r = (i // heads) * pair
            s, hh = h // hs, h % hs
            src, dst = q * quarter + r, target * quarter + r
            query = [qt[s, src + j, hh] for j in range(pair)]
            extra = [v_bias[...]] * pair
            top, total, summed = attend(
                keys[h], jnp.concatenate(query, axis=1) if pair > 1 else query[0],
                valt[h], jnp.concatenate(extra, axis=1) if pair > 1 else extra[0])
            summed = summed.astype(BF16)
            for j in range(pair):
                cut = slice(j * lat_local, (j + 1) * lat_local)
                osum[s, dst + j, hh] = summed[:, cut]
                stats[s, dst + j, hh, 0:1] = top[:, cut]
                stats[s, dst + j, hh, 1:2] = total[:, cut]
            return 0

        lax.fori_loop(0, heads * quarter // pair, body, 0)

    sent = []

    def reduce_copies(t, part, a, b, base):
        copies = []
        for s in range(N_STREAMS):
            device = partner(reduce_order[s][t])
            copies.append((
                remote(osum.at[s, a:b], orecv.at[s, base:base + b - a],
                       os_sem.at[s, t, part], or_sem.at[s, t, part], device),
                remote(stats.at[s, a:b], srecv.at[s, base:base + b - a],
                       ss_sem.at[s, t, part], sr_sem.at[s, t, part], device)))
        for o, st in copies:
            o.start()
            st.start()
        sent.extend(copies)
        return copies

    def merge(copies, a, b, base):
        for o, st in copies:
            o.wait_recv()
            st.wait_recv()

        def body(r, _):
            for h in range(heads):
                s, hh = h // hs, h % hs
                mine, theirs = stats[s, a + r, hh], srecv[s, base + r, hh]
                top = jnp.maximum(mine[0:1], theirs[0:1])
                f, g = jnp.exp2(mine[0:1] - top), jnp.exp2(theirs[0:1] - top)
                stats[s, a + r, hh, 0:1] = top
                stats[s, a + r, hh, 1:2] = mine[1:2] * f + theirs[1:2] * g
                osum[s, a + r, hh] = (
                    osum[s, a + r, hh].astype(F32) * f + orecv[s, base + r, hh].astype(F32) * g
                ).astype(BF16)
            return 0

        lax.fori_loop(0, b - a, body, 0)

    loads[5].wait()
    encode(0)
    gather_q.ready(3)
    for g in range(4, bits):
        gather_q.ready(g)
    if bits == 4:
        encode(1)
        early = reduce_copies(3, 0, 2 * quarter, 3 * quarter, quarter)
        gather_q.ready(bits)
    else:
        gather_q.ready(bits)
        encode(1)
        early = reduce_copies(bits - 1, 0, 2 * quarter, 3 * quarter, quarter)
    encode(3)
    late = reduce_copies(bits - 1, 1, 3 * quarter, n, 0)
    encode(2)
    merge(late, quarter, 2 * quarter, 0)
    base = 2 * quarter
    step = reduce_copies(bits - 2, 0, quarter, 2 * quarter, base)
    loads[6].wait()
    project(v_wpq, store_transposed(pqt))
    merge(early, 0, quarter, quarter)
    merge(step, 0, quarter, base)
    base += quarter
    for t in range(bits - 3, -1, -1):
        step = reduce_copies(t, 0, 2**t, 2 ** (t + 1), base)
        merge(step, 0, 2**t, base)
        base += 2**t
    gather_q.finish()

    attended = []
    for h in range(heads):
        s, hh = h // hs, h % hs
        attended.append((osum[s, 0, hh].astype(F32) / stats[s, 0, hh][1:2]).T.astype(BF16))
    loads[7].wait()
    partial = mm(jnp.concatenate(attended, axis=1), v_wo[...]).astype(BF16)
    msend[...] = partial
    swap = remote(msend, mrecv, x_sem.at[0], x_sem.at[1], other)
    swap.start()
    loads[8].wait()
    swap.wait()
    normed = rms_norm(msend[...].astype(F32) + mrecv[...].astype(F32))
    hidden = jax.nn.gelu(mm(normed.astype(BF16), v_wm[...]))
    lat_rows = (normed + hidden).astype(BF16)
    part_rows = lat_local // N_STREAMS
    span = width // 2
    for s in range(N_STREAMS):
        for c in range(2):
            lr[c, s, 0] = lat_rows[s * part_rows:(s + 1) * part_rows, c * span:(c + 1) * span]

    gather_l = Gather(lambda s, a, b: lr.at[core, s, a:b], hs_sem, hr_sem)
    shares = {}
    block = quarter * part_rows

    def share(g):
        gather_l.ready(g)
        a, b = group(g)
        for s in range(N_STREAMS):
            view = lr.at[core, s, a:b]
            shares[s, g] = remote(view, view, ds_sem.at[s, g], dr_sem.at[s, g], other)
            shares[s, g].start()

    def shared(g):
        for s in range(N_STREAMS):
            shares[s, g].wait_recv()

    def latent_kv(q):
        for s in range(N_STREAMS):
            at = (q * N_STREAMS + s) * block
            x = jnp.concatenate(
                [lr[c, s, q * quarter:(q + 1) * quarter].reshape(block, span) for c in range(2)],
                axis=1)
            k = mm(x, v_wlk[...]).astype(BF16)
            flipped = mm(x, v_wlv[...]).T.astype(BF16)
            for h in range(heads):
                cut = slice(h * HEAD_DIM, (h + 1) * HEAD_DIM)
                lkeys[h, at:at + block] = k[:, cut]
                lvalt[h, :, at:at + block] = flipped[cut]

    def decode_first(i, _):
        h = i % heads
        start = pl.multiple_of((i // heads) * rows, rows)
        top, total, summed = attend(
            lkeys[h, :lat // 2], pqt[h, :, pl.ds(start, rows)], lvalt[h, :, :lat // 2], None)
        dstat[h, i // heads, 0:1] = top
        dstat[h, i // heads, 1:2] = total
        dsum[h, i // heads] = summed
        return 0

    def decode(i, _):
        h = i % heads
        start = pl.multiple_of((i // heads) * rows, rows)
        top, total, summed = attend(
            lkeys[h, lat // 2:], pqt[h, :, pl.ds(start, rows)], lvalt[h, :, lat // 2:], None)
        before = dstat[h, i // heads]
        peak = jnp.maximum(top, before[0:1])
        f, g = jnp.exp2(before[0:1] - peak), jnp.exp2(top - peak)
        scaled = dsum[h, i // heads] * f + summed * g
        pa[h, pl.ds(start, rows)] = (scaled / (before[1:2] * f + total * g)).T.astype(BF16)
        return 0

    gather_l.ready(0)
    for g in range(1, bits - 1):
        share(g)
    loads[9].wait()
    loads[10].wait()
    for g in range(1, bits - 1):
        shared(g)
    latent_kv(0)
    share(bits - 1)
    shared(bits - 1)
    latent_kv(1)
    lax.fori_loop(0, pos // rows * heads, decode_first, 0)
    share(bits)
    shared(bits)
    latent_kv(2)
    latent_kv(3)

    half = pos // 2
    loads[11].wait()

    def terms(start, size):
        joined = jnp.concatenate([pa[h, pl.ds(start, size)] for h in range(heads)], axis=1)
        return mm(joined, v_wpo[...])

    per_half = half // rows
    theirs = (1 - core) * per_half
    mine = core * per_half
    swaps = []
    for i in range(per_half):
        lax.fori_loop((theirs + i) * heads, (theirs + i + 1) * heads, decode, 0)
        start = pl.multiple_of((theirs + i) * rows, rows)
        tsend[i] = terms(start, rows).astype(BF16)
        copy = remote(tsend.at[i], trecv.at[i], x_sem.at[2 + 2 * i], x_sem.at[3 + 2 * i], other)
        copy.start()
        swaps.append(copy)
    for i in range(per_half):
        lax.fori_loop((mine + i) * heads, (mine + i + 1) * heads, decode, 0)
        start = pl.multiple_of((mine + i) * rows, rows)
        own_terms = terms(start, rows).astype(BF16).astype(F32)
        swaps[i].wait_recv()
        out[i * rows:(i + 1) * rows] = rms_norm(own_terms + trecv[i].astype(F32)).astype(BF16)
    for copy in swaps:
        copy.wait_send()
    for o, st in sent:
        o.wait_send()
        st.wait_send()
    gather_l.finish()
    for copy in shares.values():
        copy.wait_send()


def per_device(n, inputs, valid_blocks, latents, *weights):
    pos, width = inputs.shape
    lat_local = latents.shape[0]
    columns = weights[0].shape[1]
    heads = columns // HEAD_DIM
    hs = heads // N_STREAMS
    lat = n * lat_local
    bits = n.bit_length() - 1
    rows = min(pos, 256)
    per_half = pos // 2 // rows
    block = pos // valid_blocks.shape[0]
    bias = jnp.where(jnp.repeat(valid_blocks, block) > 0, 0.0, masked_score).astype(F32)
    bias = jnp.broadcast_to(bias[:, None], (pos, lat_local))
    operands = (inputs, bias, latents) + weights
    landed = [pltpu.VMEM(a.shape, a.dtype) for a in operands]
    dma = pltpu.SemaphoreType.DMA
    n_recv = n
    scratch = landed + [
        pltpu.VMEM((N_STREAMS, n, hs, HEAD_DIM, lat_local), BF16),
        pltpu.VMEM((heads, pos, HEAD_DIM), BF16),
        pltpu.VMEM((heads, HEAD_DIM, pos), BF16),
        pltpu.VMEM((heads, HEAD_DIM, pos), BF16),
        pltpu.VMEM((N_STREAMS, n, hs, HEAD_DIM, lat_local), BF16),
        pltpu.VMEM((N_STREAMS, n, hs, 2, lat_local), F32),
        pltpu.VMEM((N_STREAMS, n_recv, hs, HEAD_DIM, lat_local), BF16),
        pltpu.VMEM((N_STREAMS, n_recv, hs, 2, lat_local), F32),
        pltpu.VMEM((2, N_STREAMS, n, lat_local // N_STREAMS, width // 2), BF16),
        pltpu.VMEM((heads, lat, HEAD_DIM), BF16),
        pltpu.VMEM((heads, HEAD_DIM, lat), BF16),
        pltpu.VMEM((heads, pos, HEAD_DIM), BF16),
        pltpu.VMEM((heads, pos // rows, 2, rows), F32),
        pltpu.VMEM((heads, pos // rows, HEAD_DIM, rows), F32),
        pltpu.VMEM((per_half, rows, width), BF16),
        pltpu.VMEM((per_half, rows, width), BF16),
        pltpu.VMEM((lat_local, width), BF16),
        pltpu.VMEM((lat_local, width), BF16),
        dma((len(operands),)),
        dma((N_STREAMS, bits, bits)),
        dma((N_STREAMS, bits, bits)),
        dma((N_STREAMS, bits, bits)),
        dma((N_STREAMS, bits, bits)),
        dma((N_STREAMS, bits + 1)),
        dma((N_STREAMS, bits + 1)),
        dma((N_STREAMS, bits, 2)),
        dma((N_STREAMS, bits, 2)),
        dma((N_STREAMS, bits, 2)),
        dma((N_STREAMS, bits, 2)),
        dma((2 + 2 * per_half,)),
    ]
    return pl.pallas_call(
        functools.partial(kernel, n),
        out_shape=jax.ShapeDtypeStruct((pos // 2, width), BF16),
        in_specs=[pl.BlockSpec(memory_space=pl.ANY)] * len(operands),
        out_specs=pl.BlockSpec(memory_space=pltpu.VMEM),
        scratch_shapes=scratch,
        compiler_params=pltpu.CompilerParams(
            collective_id=0, has_side_effects=True, vmem_limit_bytes=60 * 1024 * 1024),
        name="perceiver",
    )(*operands)


def solution(mesh):
    placed = (
        P("pos", None),
        P("pos"),
        P("pos", None),
        P(None, "head"),
        P(None, "head"),
        P(None, "head"),
        P("head", None),
        P(),
        P(None, "head"),
        P(None, "head"),
        P(None, "head"),
        P("head", None),
    )
    return jax.shard_map(
        functools.partial(per_device, mesh.shape["pos"]), mesh=mesh, in_specs=placed,
        out_specs=P(("pos", "head"), None), check_vma=False
    )
```
